512 devices in a mesh: dp: 64 (over z, x_hi, core), tensor: 8 (over y, x_lo).
Axes of the slice: x: 4 (x_hi: 2, x_lo: 2; x = x_hi * 2 + x_lo), y: 4, z: 16, core: 2. Of those that a mesh axis runs over, the one named last changes fastest.
Arguments:
- acts: bfloat16 [32768, 8192], P('dp', 'tensor'), may hold values from -6 to 6
- cotangent: bfloat16 [32768, 14336], P('dp', 'tensor'), may hold values from -0.032958984 to 0.032958984
- basis: bfloat16 [8192, 512], P('tensor'), may hold values from -0.375 to 0.375
- weight: bfloat16 [8192, 14336], P('dp', 'tensor'), may hold values from -6 to 6
- first_moment: float32 [512, 14336], P('dp', 'tensor'), may hold values from -12 to 12
- second_moment: float32 [512, 14336], P('dp', 'tensor'), may hold values from 1 to 32
Outputs:
- new_weight: bfloat16 [8192, 14336], P('dp', 'tensor')
- first_new: float32 [512, 14336], P('dp', 'tensor')
- second_new: float32 [512, 14336], P('dp', 'tensor')
The draws below stay inside these ranges and needn't reach their ends.
All inputs are finite; a program needn't handle non-finite values.
Results may differ from the reference program's by a relative error of at most 0.0033.
Values may be sent and summed in bfloat16 or wider, within the bound.
No kernel may reach another device: no remote copies, remote signals or barrier semaphores. Data moves between devices by JAX's collectives and lax.ppermute only.
A program may use at most 64 MiB of HBM per device.

```python
import math
import jax
import jax.numpy as jnp

D = 8192
F = 14336
R = 512
TOKENS = 32768


def steps_of(stream_key, extent, cuts, smallest, largest):
    def one(position, shards_of):
        steps = jax.random.uniform(jax.random.fold_in(jax.random.fold_in(stream_key, 6), position), (shards_of,), jnp.float32, smallest / len(cuts), largest / len(cuts))
        return jnp.repeat(jnp.exp(steps), extent[position] // shards_of).reshape((-1,) + (1,) * (len(extent) - position - 1))

    gain = one(*cuts[0])
    for cut in cuts[1:]:
        gain = gain * one(*cut)
    return gain


def centred(rng, shape, spread, limit, split=(), held_as=jnp.bfloat16):
    array = jax.random.normal(rng, shape, jnp.float32) * spread
    if len(split) > 0:
        array = steps_of(rng, shape, split, -0.22, 0.18) * array
    return jnp.clip(array, min=-limit, max=limit).astype(held_as)


def setup_inputs(seed: int = 0) -> dict:
    arg_keys = jax.random.split(jax.random.key(seed), 7)
    return {
        "acts": centred(arg_keys[0], (TOKENS, D), 1.0, 6.0, ((0, 64), (1, 8))),
        "cotangent": centred(arg_keys[1], (TOKENS, F), (1.0 / TOKENS ** 0.5), 0.032958984, ((0, 64), (1, 8))),
        "basis": centred(arg_keys[2], (D, R), (R // 2) ** -0.5, 0.375, ((0, 8),)),
        "weight": centred(arg_keys[3], (D, F), 1.0, 6.0, ((0, 64), (1, 8))),
        "first_moment": centred(arg_keys[4], (R, F), 2.0, 12.0, ((0, 64), (1, 8)), jnp.float32),
        "second_moment": jnp.clip(jnp.exp(math.log(32.0) - 3.465736 * jax.random.uniform(arg_keys[5], (R, F), jnp.float32) ** steps_of(arg_keys[5], (R, F), ((0, 64), (1, 8)), -0.2, 0.2)), 1.0, 32.0),
    }


BETA_ONE = 0.9
BETA_TWO = 0.95
EPSILON = 1e-08
STEP_SCALE = 0.5

def reference(acts, cotangent, basis, weight, first_moment, second_moment):
    projected = jnp.dot(acts, basis, preferred_element_type=jnp.float32).astype(jnp.bfloat16)
    low_grad = jnp.dot(projected.T, cotangent, preferred_element_type=jnp.float32)
    first_new = BETA_ONE * first_moment + (1.0 - BETA_ONE) * low_grad
    second_new = BETA_TWO * second_moment + (1.0 - BETA_TWO) * low_grad * low_grad
    normed = (first_new / (jnp.sqrt(second_new) + EPSILON)).astype(jnp.bfloat16)
    update = jnp.dot(basis, normed, preferred_element_type=jnp.float32)
    new_weight = (weight.astype(jnp.float32) - STEP_SCALE * update).astype(jnp.bfloat16)
    return (new_weight, first_new, second_new)
```

```python
import jax
import jax.numpy as jnp
import numpy as np
from jax import lax
from jax.sharding import Mesh
from jax.sharding import PartitionSpec as P

BETA_ONE = 0.9
BETA_TWO = 0.95
EPSILON = 1e-08
STEP_SCALE = 0.5

Z_HI, Z_LO, X_HI, CORE = 8, 2, 2, 2
DP = ("z_hi", "z_lo", "x_hi", "core")
TENSOR = 8


def dot(lhs, rhs, lhs_dim, rhs_dim):
    return lax.dot_general(
        lhs,
        rhs,
        (((lhs_dim,), (rhs_dim,)), ((), ())),
        preferred_element_type=jnp.float32,
    )


def scatter_sum(value, axes, count):
    rows, columns = value.shape
    blocks = value.reshape(count, rows // count, columns)
    blocks = lax.all_to_all(blocks, axes, 0, 0, tiled=True)
    return jnp.sum(blocks.astype(jnp.float32), axis=0)


def spread_rows(value, axes, count):
    copies = jnp.broadcast_to(value[None], (count,) + value.shape)
    blocks = lax.all_to_all(copies, axes, 0, 0, tiled=True)
    return blocks.reshape(count * value.shape[0], value.shape[1])


def swap_cores(value):
    return lax.ppermute(value, "core", [(0, 1), (1, 0)])


def rank_order(rank):
    rows = np.arange(rank).reshape(Z_HI, Z_LO, X_HI, CORE, -1)
    return rows.transpose(3, 1, 2, 0, 4).reshape(-1)


def basis_routes():
    routes = []
    for z in range(Z_HI * Z_LO):
        for rest in range(X_HI * CORE):
            for shard in range(TENSOR):
                target_z = shard * Z_LO + z % Z_LO
                target_tensor = (z // Z_LO - shard) % TENSOR
                source = (z * X_HI * CORE + rest) * TENSOR + shard
                target = (target_z * X_HI * CORE + rest) * TENSOR + target_tensor
                routes.append((source, target))
    return routes


def local(acts, cotangent, basis, weight, first_moment, second_moment):
    rank = basis.shape[1]
    half = rank // 2
    core = lax.axis_index("core")
    order = rank_order(rank)
    inverse = np.argsort(order)
    place = (
        lax.broadcasted_iota(jnp.int32, (rank, rank), 1)
        == jnp.asarray(inverse, jnp.int32)[:, None]
    ).astype(jnp.bfloat16)
    basis = dot(basis, place, 1, 0).astype(jnp.bfloat16)

    row_block = weight.shape[0]
    spot = (lax.axis_index("z_lo") * X_HI + lax.axis_index("x_hi")) * CORE + core
    row_basis = lax.ppermute(
        lax.dynamic_slice_in_dim(basis, spot * row_block, row_block, 0),
        DP + ("tensor",),
        basis_routes(),
    )

    partial_value = dot(basis, acts, 0, 1).astype(jnp.bfloat16)
    projected = scatter_sum(partial_value, "tensor", TENSOR).astype(jnp.bfloat16)
    projected, row_basis = lax.optimization_barrier((projected, row_basis))
    projected = spread_rows(projected, "tensor", TENSOR)

    theirs = lax.dynamic_slice_in_dim(projected, (1 - core) * half, half, 0)
    ours = lax.dynamic_slice_in_dim(projected, core * half, half, 0)
    got = swap_cores(dot(theirs, cotangent, 1, 0).astype(jnp.bfloat16))
    low_grad = dot(ours, cotangent, 1, 0) + got.astype(jnp.float32)
    low_grad = scatter_sum(low_grad.astype(jnp.bfloat16), ("z_lo", "x_hi"), 4)
    low_grad = scatter_sum(low_grad.astype(jnp.bfloat16), "z_hi", Z_HI)

    first_new = BETA_ONE * first_moment + (1.0 - BETA_ONE) * low_grad
    second_new = BETA_TWO * second_moment + (1.0 - BETA_TWO) * low_grad * low_grad
    normed = (first_new / (jnp.sqrt(second_new) + EPSILON)).astype(jnp.bfloat16)

    normed = spread_rows(normed, "z_hi", Z_HI)
    normed = spread_rows(normed, ("z_lo", "x_hi"), 4)
    other = swap_cores(normed)
    own_basis = lax.dynamic_slice_in_dim(row_basis, core * half, half, 1)
    other_basis = lax.dynamic_slice_in_dim(row_basis, (1 - core) * half, half, 1)
    update = dot(own_basis, normed, 1, 0) + dot(other_basis, other, 1, 0)
    new_weight = (weight.astype(jnp.float32) - STEP_SCALE * update).astype(jnp.bfloat16)
    return (new_weight, first_new, second_new)


def solution(mesh):
    devices = mesh.devices.reshape(Z_HI, Z_LO, X_HI, CORE, TENSOR)
    split = Mesh(devices, DP + ("tensor",))
    placed = (
        P(DP, "tensor"),
        P(DP, "tensor"),
        P("tensor", None),
        P(DP, "tensor"),
        P(DP, "tensor"),
        P(DP, "tensor"),
    )
    return jax.shard_map(
        local,
        mesh=split,
        in_specs=placed,
        out_specs=(P(DP, "tensor"), P(DP, "tensor"), P(DP, "tensor")),
        check_vma=False,
    )
```

```python
import jax
import jax.numpy as jnp
import numpy as np
from jax import lax
from jax.sharding import Mesh
from jax.sharding import PartitionSpec as P

BETA_ONE = 0.9
BETA_TWO = 0.95
EPSILON = 1e-08
STEP_SCALE = 0.5

Z_HI, Z_LO, X_HI, CORE = 8, 2, 2, 2
DP = ("z_hi", "z_lo", "x_hi", "core")
TENSOR = 8


def dot(lhs, rhs, lhs_dim, rhs_dim):
    return lax.dot_general(
        lhs,
        rhs,
        (((lhs_dim,), (rhs_dim,)), ((), ())),
        preferred_element_type=jnp.float32,
    )


def scatter_sum(blocks, axes):
    blocks = lax.all_to_all(blocks, axes, 0, 0, tiled=True)
    return jnp.sum(blocks.astype(jnp.float32), axis=0)


def spread_rows(value, axes, count):
    copies = jnp.broadcast_to(value[None], (count,) + value.shape)
    return lax.all_to_all(copies, axes, 0, 0, tiled=True)


def swap_cores(value):
    return lax.ppermute(value, "core", [(0, 1), (1, 0)])


def rank_order(rank):
    rows = np.arange(rank).reshape(Z_HI, Z_LO, X_HI, CORE, -1)
    return rows.transpose(3, 1, 2, 0, 4).reshape(-1)


def local(acts, cotangent, basis, weight, first_moment, second_moment):
    rank = basis.shape[1]
    half = rank // 2
    core = lax.axis_index("core")
    order = rank_order(rank)
    inverse = np.argsort(order)
    place = (
        lax.broadcasted_iota(jnp.int32, (rank, rank), 1)
        == jnp.asarray(inverse, jnp.int32)[:, None]
    ).astype(jnp.bfloat16)
    basis = dot(basis, place, 1, 0).astype(jnp.bfloat16)

    partner_cotangent = swap_cores(cotangent)

    columns = cotangent.shape[1]
    row_block = weight.shape[0]
    piece = row_block // (CORE * TENSOR)
    spot = lax.axis_index("z_lo") * X_HI + lax.axis_index("x_hi")
    dealt = lax.dynamic_slice_in_dim(basis, spot * CORE * row_block, CORE * row_block, 0)
    dealt = dealt.reshape(CORE, CORE, TENSOR, piece, rank)
    dealt = lax.dynamic_index_in_dim(dealt, core, 1, False)
    mine = lax.axis_index("tensor") == lax.axis_index("z_hi")
    dealt = jnp.where(mine, dealt, 0).astype(jnp.bfloat16)

    partial_value = dot(basis, acts, 0, 1).astype(jnp.bfloat16)
    share = half // TENSOR
    both = jnp.concatenate([partial_value.reshape(CORE, TENSOR, share, -1), dealt], axis=2)
    both = scatter_sum(both.transpose(1, 0, 2, 3), "tensor").astype(jnp.bfloat16)
    both = jnp.broadcast_to(both[:, None], (CORE, TENSOR) + both.shape[1:])
    both = both.reshape((CORE * TENSOR,) + both.shape[2:])
    both = lax.all_to_all(both, ("core", "tensor"), 0, 0, tiled=True)
    projected = both[:, :share].reshape(CORE, half, -1)
    row_basis = both[:, share:].reshape(row_block, rank)

    low_grad = dot(
        lax.dynamic_index_in_dim(projected, core, 0, False), cotangent, 1, 0
    ) + dot(
        lax.dynamic_index_in_dim(projected, 1 - core, 0, False), partner_cotangent, 1, 0
    )
    low_grad = low_grad.astype(jnp.bfloat16).reshape(Z_LO * X_HI, -1, columns)
    low_grad = scatter_sum(low_grad, ("z_lo", "x_hi"))
    low_grad = low_grad.astype(jnp.bfloat16).reshape(Z_HI, -1, columns)
    low_grad = scatter_sum(low_grad, "z_hi")

    first_new = BETA_ONE * first_moment + (1.0 - BETA_ONE) * low_grad
    second_new = BETA_TWO * second_moment + (1.0 - BETA_TWO) * low_grad * low_grad
    normed = (first_new / (jnp.sqrt(second_new) + EPSILON)).astype(jnp.bfloat16)

    normed = spread_rows(normed, "z_hi", Z_HI).reshape(-1, columns)
    normed = spread_rows(normed, ("z_lo", "x_hi"), Z_LO * X_HI).reshape(half, columns)
    other = swap_cores(normed)
    own_basis = lax.dynamic_slice_in_dim(row_basis, core * half, half, 1)
    other_basis = lax.dynamic_slice_in_dim(row_basis, (1 - core) * half, half, 1)
    update = dot(own_basis, normed, 1, 0) + dot(other_basis, other, 1, 0)
    new_weight = (weight.astype(jnp.float32) - STEP_SCALE * update).astype(jnp.bfloat16)
    return (new_weight, first_new, second_new)


def solution(mesh):
    devices = mesh.devices.reshape(Z_HI, Z_LO, X_HI, CORE, TENSOR)
    split = Mesh(devices, DP + ("tensor",))
    placed = (
        P(DP, "tensor"),
        P(DP, "tensor"),
        P("tensor", None),
        P(DP, "tensor"),
        P(DP, "tensor"),
        P(DP, "tensor"),
    )
    return jax.shard_map(
        local,
        mesh=split,
        in_specs=placed,
        out_specs=(P(DP, "tensor"), P(DP, "tensor"), P(DP, "tensor")),
        check_vma=False,
    )
```

```python
import jax
import jax.numpy as jnp
import numpy as np
from jax import lax
from jax.experimental import pallas as pl
from jax.experimental.pallas import tpu as pltpu
from jax.sharding import Mesh
from jax.sharding import PartitionSpec as P

BETA_ONE = 0.9
BETA_TWO = 0.95
EPSILON = 1e-08
STEP_SCALE = 0.5

Z_HI, Z_LO, X_HI, CORE = 8, 2, 2, 2
DP = ("z_hi", "z_lo", "x_hi", "core")
TENSOR = 8
TILE = 896
TOKEN_TILE = 256


def dot(lhs, rhs, lhs_dim, rhs_dim):
    return lax.dot_general(
        lhs,
        rhs,
        (((lhs_dim,), (rhs_dim,)), ((), ())),
        preferred_element_type=jnp.float32,
    )


def scatter_sum(blocks, axes):
    blocks = lax.all_to_all(blocks, axes, 0, 0, tiled=True)
    return jnp.sum(blocks.astype(jnp.float32), axis=0)


def spread_rows(value, axes, count):
    copies = jnp.broadcast_to(value[None], (count,) + value.shape)
    return lax.all_to_all(copies, axes, 0, 0, tiled=True)


def swap_cores(value):
    return lax.ppermute(value, "core", [(0, 1), (1, 0)])


def rank_order(rank):
    rows = np.arange(rank).reshape(Z_HI, Z_LO, X_HI, CORE, -1)
    return rows.transpose(3, 1, 2, 0, 4).reshape(-1)


def first_product(turned, acts, where, row_block):
    rank, features = turned.shape
    tokens = acts.shape[0]
    share = rank // (CORE * TENSOR)
    deal = row_block // CORE
    piece = deal // TENSOR

    def kernel(where_ref, turned_ref, acts_ref, out_ref):
        dealt = []
        for c in range(CORE):
            start = pl.multiple_of((where_ref[1] * CORE + c) * row_block, row_block)
            some = turned_ref[:, pl.ds(start, row_block)].astype(jnp.float32).T
            some = jnp.where(where_ref[0] == 0, some[:deal], some[deal:])
            dealt.append(jnp.where(where_ref[2] == 1, some, 0.0))
        for i in range(tokens // TOKEN_TILE):
            part = slice(i * TOKEN_TILE, (i + 1) * TOKEN_TILE)
            value = dot(turned_ref[...], acts_ref[part], 1, 1)
            for c in range(CORE):
                for t in range(TENSOR):
                    top = (c * TENSOR + t) * share
                    low = dealt[c][t * piece : (t + 1) * piece, part]
                    block = jnp.concatenate([value[top : top + share], low], axis=0)
                    out_ref[t, c, :, part] = block.astype(jnp.bfloat16)

    out = (TENSOR, CORE, share + piece, tokens)
    return pl.pallas_call(
        kernel,
        in_specs=[pl.BlockSpec(memory_space=pltpu.SMEM)]
        + [pl.BlockSpec(memory_space=pltpu.VMEM)] * 2,
        out_specs=pl.BlockSpec(memory_space=pltpu.VMEM),
        out_shape=jax.ShapeDtypeStruct(out, jnp.bfloat16),
        cost_estimate=pl.CostEstimate(
            flops=2 * rank * features * tokens,
            bytes_accessed=2 * (turned.size + acts.size + rank * tokens),
            transcendentals=0,
        ),
        compiler_params=pltpu.CompilerParams(vmem_limit_bytes=14 * 2**20),
    )(where, turned, acts)


def sum_and_copy(blocks):
    senders, cores, rows, columns = blocks.shape

    def kernel(in_ref, out_ref):
        for c in range(cores):
            total = in_ref[0, c].astype(jnp.float32)
            for t in range(1, senders):
                total += in_ref[t, c].astype(jnp.float32)
            total = total.astype(jnp.bfloat16)
            for t in range(senders):
                out_ref[c * senders + t] = total

    return pl.pallas_call(
        kernel,
        in_specs=[pl.BlockSpec(memory_space=pltpu.VMEM)],
        out_specs=pl.BlockSpec(memory_space=pltpu.VMEM),
        out_shape=jax.ShapeDtypeStruct((cores * senders, rows, columns), jnp.bfloat16),
        cost_estimate=pl.CostEstimate(
            flops=blocks.size, bytes_accessed=4 * blocks.size, transcendentals=0
        ),
        compiler_params=pltpu.CompilerParams(vmem_limit_bytes=8 * 2**20),
    )(blocks)


def rank_product(both, cotangent, partner_cotangent, core, share):
    blocks, rows, tokens = both.shape
    columns = cotangent.shape[1]
    count = blocks // CORE

    def kernel(core_ref, both_ref, own_ref, partner_ref, out_ref):
        me = core_ref[0]
        ours = both_ref[pl.ds(me * count, count), :share, :]
        theirs = both_ref[pl.ds((1 - me) * count, count), :share, :]
        total = dot(ours.reshape(count * share, tokens), own_ref[...], 1, 0)
        total += dot(theirs.reshape(count * share, tokens), partner_ref[...], 1, 0)
        out_ref[...] = total.astype(jnp.bfloat16)

    tile = pl.BlockSpec((tokens, TILE), lambda i: (0, i))
    return pl.pallas_call(
        kernel,
        grid=(columns // TILE,),
        in_specs=[
            pl.BlockSpec(memory_space=pltpu.SMEM),
            pl.BlockSpec(both.shape, lambda i: (0, 0, 0)),
            tile,
            tile,
        ],
        out_specs=pl.BlockSpec((count * share, TILE), lambda i: (0, i)),
        out_shape=jax.ShapeDtypeStruct((count * share, columns), jnp.bfloat16),
        cost_estimate=pl.CostEstimate(
            flops=4 * count * share * tokens * columns,
            bytes_accessed=2 * (both.size + 2 * cotangent.size + count * share * columns),
            transcendentals=0,
        ),
        compiler_params=pltpu.CompilerParams(vmem_limit_bytes=10 * 2**20),
    )(core.astype(jnp.int32).reshape(1), both, cotangent, partner_cotangent)


def local(acts, cotangent, basis, weight, first_moment, second_moment):
    rank = basis.shape[1]
    half = rank // 2
    core = lax.axis_index("core")
    share = half // TENSOR
    columns = cotangent.shape[1]
    row_block = weight.shape[0]
    place = jnp.asarray(np.eye(rank)[rank_order(rank)], jnp.bfloat16)

    spot = lax.axis_index("z_lo") * X_HI + lax.axis_index("x_hi")
    mine = lax.axis_index("tensor") == lax.axis_index("z_hi")
    where = jnp.stack([core, spot, mine.astype(jnp.int32)]).astype(jnp.int32)
    turned = dot(place, basis, 1, 1).astype(jnp.bfloat16)
    both = first_product(turned, acts, where, row_block)
    both = lax.all_to_all(both, "tensor", 0, 0, tiled=True)
    both, cotangent = lax.optimization_barrier((both, cotangent))

    partner_cotangent = swap_cores(cotangent)
    both = sum_and_copy(both)
    both = lax.all_to_all(both, ("core", "tensor"), 0, 0, tiled=True)
    row_basis = both[:, share:].reshape(row_block, rank)

    low_grad = rank_product(both, cotangent, partner_cotangent, core, share)
    low_grad = low_grad.reshape(Z_LO * X_HI, -1, columns)
    low_grad = scatter_sum(low_grad, ("z_lo", "x_hi"))
    low_grad = low_grad.astype(jnp.bfloat16).reshape(Z_HI, -1, columns)
    low_grad = scatter_sum(low_grad, "z_hi")

    first_new = BETA_ONE * first_moment + (1.0 - BETA_ONE) * low_grad
    second_new = BETA_TWO * second_moment + (1.0 - BETA_TWO) * low_grad * low_grad
    normed = (first_new / (jnp.sqrt(second_new) + EPSILON)).astype(jnp.bfloat16)

    normed = spread_rows(normed, "z_hi", Z_HI).reshape(-1, columns)
    normed = spread_rows(normed, ("z_lo", "x_hi"), Z_LO * X_HI).reshape(half, columns)
    other = swap_cores(normed)
    own_basis = lax.dynamic_slice_in_dim(row_basis, core * half, half, 1)
    other_basis = lax.dynamic_slice_in_dim(row_basis, (1 - core) * half, half, 1)
    update = dot(own_basis, normed, 1, 0) + dot(other_basis, other, 1, 0)
    new_weight = (weight.astype(jnp.float32) - STEP_SCALE * update).astype(jnp.bfloat16)
    return (new_weight, first_new, second_new)


def solution(mesh):
    devices = mesh.devices.reshape(Z_HI, Z_LO, X_HI, CORE, TENSOR)
    split = Mesh(devices, DP + ("tensor",))
    placed = (
        P(DP, "tensor"),
        P(DP, "tensor"),
        P("tensor", None),
        P(DP, "tensor"),
        P(DP, "tensor"),
        P(DP, "tensor"),
    )
    return jax.shard_map(
        local,
        mesh=split,
        in_specs=placed,
        out_specs=(P(DP, "tensor"), P(DP, "tensor"), P(DP, "tensor")),
        check_vma=False,
    )
```

```python
import jax
import jax.numpy as jnp
import numpy as np
from jax import lax
from jax.experimental import pallas as pl
from jax.experimental.pallas import tpu as pltpu
from jax.sharding import Mesh
from jax.sharding import PartitionSpec as P

BETA_ONE = 0.9
BETA_TWO = 0.95
EPSILON = 1e-08
STEP_SCALE = 0.5

Z_HI, Z_LO, X_HI, CORE = 8, 2, 2, 2
DP = ("z_hi", "z_lo", "x_hi", "core")
TENSOR = 8
TILE = 256
TOKEN_TILE = 256


def dot(lhs, rhs, lhs_dim, rhs_dim):
    return lax.dot_general(
        lhs,
        rhs,
        (((lhs_dim,), (rhs_dim,)), ((), ())),
        preferred_element_type=jnp.float32,
    )


def scatter_sum(blocks, axes):
    blocks = lax.all_to_all(blocks, axes, 0, 0, tiled=True)
    return jnp.sum(blocks.astype(jnp.float32), axis=0)


def spread_rows(value, axes, count):
    copies = jnp.broadcast_to(value[None], (count,) + value.shape)
    return lax.all_to_all(copies, axes, 0, 0, tiled=True)


def swap_cores(value):
    return lax.ppermute(value, "core", [(0, 1), (1, 0)])


def rank_order(rank):
    rows = np.arange(rank).reshape(Z_HI, Z_LO, X_HI, CORE, -1)
    return rows.transpose(3, 2, 1, 0, 4).reshape(-1)


def first_product(turned, acts, where, row_block):
    rank, features = turned.shape
    tokens = acts.shape[0]
    share = rank // (CORE * TENSOR)
    deal = row_block // CORE
    piece = deal // TENSOR

    def kernel(where_ref, turned_ref, acts_ref, out_ref):
        dealt = []
        for c in range(CORE):
            start = pl.multiple_of((where_ref[1] * CORE + c) * row_block, row_block)
            some = turned_ref[:, pl.ds(start, row_block)].astype(jnp.float32).T
            some = jnp.where(where_ref[0] == 0, some[:deal], some[deal:])
            dealt.append(jnp.where(where_ref[2] == 1, some, 0.0))
        for i in range(tokens // TOKEN_TILE):
            part = slice(i * TOKEN_TILE, (i + 1) * TOKEN_TILE)
            value = dot(turned_ref[...], acts_ref[part], 1, 1)
            for c in range(CORE):
                for t in range(TENSOR):
                    top = (c * TENSOR + t) * share
                    low = dealt[c][t * piece : (t + 1) * piece, part]
                    block = jnp.concatenate([value[top : top + share], low], axis=0)
                    out_ref[t, c, :, part] = block.astype(jnp.bfloat16)

    out = (TENSOR, CORE, share + piece, tokens)
    return pl.pallas_call(
        kernel,
        in_specs=[pl.BlockSpec(memory_space=pltpu.SMEM)]
        + [pl.BlockSpec(memory_space=pltpu.VMEM)] * 2,
        out_specs=pl.BlockSpec(memory_space=pltpu.VMEM),
        out_shape=jax.ShapeDtypeStruct(out, jnp.bfloat16),
        cost_estimate=pl.CostEstimate(
            flops=2 * rank * features * tokens,
            bytes_accessed=2 * (turned.size + acts.size + rank * tokens),
            transcendentals=0,
        ),
        compiler_params=pltpu.CompilerParams(vmem_limit_bytes=14 * 2**20),
    )(where, turned, acts)


def sum_and_copy(blocks):
    senders, cores, rows, columns = blocks.shape

    def kernel(in_ref, out_ref):
        for c in range(cores):
            total = in_ref[0, c].astype(jnp.float32)
            for t in range(1, senders):
                total += in_ref[t, c].astype(jnp.float32)
            total = total.astype(jnp.bfloat16)
            for t in range(senders):
                out_ref[c * senders + t] = total

    return pl.pallas_call(
        kernel,
        in_specs=[pl.BlockSpec(memory_space=pltpu.VMEM)],
        out_specs=pl.BlockSpec(memory_space=pltpu.VMEM),
        out_shape=jax.ShapeDtypeStruct((cores * senders, rows, columns), jnp.bfloat16),
        cost_estimate=pl.CostEstimate(
            flops=blocks.size, bytes_accessed=4 * blocks.size, transcendentals=0
        ),
        compiler_params=pltpu.CompilerParams(vmem_limit_bytes=8 * 2**20),
    )(blocks)


def rank_product(both, cotangent, partner_cotangent, core, share):
    blocks, rows, tokens = both.shape
    columns = cotangent.shape[1]
    count = blocks // CORE

    def kernel(core_ref, both_ref, own_ref, partner_ref, out_ref):
        me = core_ref[0]
        ours = both_ref[pl.ds(me * count, count), :share, :]
        theirs = both_ref[pl.ds((1 - me) * count, count), :share, :]
        ours = ours.reshape(count * share, tokens)
        theirs = theirs.reshape(count * share, tokens)
        for start in range(0, columns, TILE):
            part = slice(start, start + TILE)
            total = dot(ours, own_ref[:, part], 1, 0)
            total += dot(theirs, partner_ref[:, part], 1, 0)
            out_ref[:, part] = total.astype(jnp.bfloat16)

    return pl.pallas_call(
        kernel,
        in_specs=[pl.BlockSpec(memory_space=pltpu.SMEM)]
        + [pl.BlockSpec(memory_space=pltpu.VMEM)] * 3,
        out_specs=pl.BlockSpec(memory_space=pltpu.VMEM),
        out_shape=jax.ShapeDtypeStruct((count * share, columns), jnp.bfloat16),
        cost_estimate=pl.CostEstimate(
            flops=4 * count * share * tokens * columns,
            bytes_accessed=2 * (both.size + 2 * cotangent.size + count * share * columns),
            transcendentals=0,
        ),
        compiler_params=pltpu.CompilerParams(vmem_limit_bytes=12 * 2**20),
    )(core.astype(jnp.int32).reshape(1), both, cotangent, partner_cotangent)


def local(acts, cotangent, basis, weight, first_moment, second_moment):
    rank = basis.shape[1]
    half = rank // 2
    core = lax.axis_index("core")
    share = half // TENSOR
    columns = cotangent.shape[1]
    row_block = weight.shape[0]
    place = jnp.asarray(np.eye(rank)[rank_order(rank)], jnp.bfloat16)

    spot = lax.axis_index("z_lo") * X_HI + lax.axis_index("x_hi")
    mine = lax.axis_index("tensor") == lax.axis_index("z_hi")
    where = jnp.stack([core, spot, mine.astype(jnp.int32)]).astype(jnp.int32)
    turned = dot(place, basis, 1, 1).astype(jnp.bfloat16)
    both = first_product(turned, acts, where, row_block)
    both = lax.all_to_all(both, "tensor", 0, 0, tiled=True)
    both, cotangent = lax.optimization_barrier((both, cotangent))

    partner_cotangent = swap_cores(cotangent)
    both = sum_and_copy(both)
    both = lax.all_to_all(both, ("core", "tensor"), 0, 0, tiled=True)
    row_basis = both[:, share:].reshape(row_block, rank)

    low_grad = rank_product(both, cotangent, partner_cotangent, core, share)
    low_grad = low_grad.reshape(Z_LO * X_HI, -1, columns)
    low_grad = scatter_sum(low_grad, ("x_hi", "z_lo"))
    low_grad = low_grad.astype(jnp.bfloat16).reshape(Z_HI, -1, columns)
    low_grad = scatter_sum(low_grad, "z_hi")

    first_new = BETA_ONE * first_moment + (1.0 - BETA_ONE) * low_grad
    second_new = BETA_TWO * second_moment + (1.0 - BETA_TWO) * low_grad * low_grad
    normed = (first_new / (jnp.sqrt(second_new) + EPSILON)).astype(jnp.bfloat16)

    normed = spread_rows(normed, "z_hi", Z_HI).reshape(-1, columns)
    normed = spread_rows(normed, ("x_hi", "z_lo"), Z_LO * X_HI).reshape(half, columns)
    other = swap_cores(normed)
    own_basis = lax.dynamic_slice_in_dim(row_basis, core * half, half, 1)
    other_basis = lax.dynamic_slice_in_dim(row_basis, (1 - core) * half, half, 1)
    update = dot(own_basis, normed, 1, 0) + dot(other_basis, other, 1, 0)
    new_weight = (weight.astype(jnp.float32) - STEP_SCALE * update).astype(jnp.bfloat16)
    return (new_weight, first_new, second_new)


def solution(mesh):
    devices = mesh.devices.reshape(Z_HI, Z_LO, X_HI, CORE, TENSOR)
    split = Mesh(devices, DP + ("tensor",))
    placed = (
        P(DP, "tensor"),
        P(DP, "tensor"),
        P("tensor", None),
        P(DP, "tensor"),
        P(DP, "tensor"),
        P(DP, "tensor"),
    )
    return jax.shard_map(
        local,
        mesh=split,
        in_specs=placed,
        out_specs=(P(DP, "tensor"), P(DP, "tensor"), P(DP, "tensor")),
        check_vma=False,
    )
```

```python
import jax
import jax.numpy as jnp
import numpy as np
from jax import lax
from jax.experimental import pallas as pl
from jax.experimental.pallas import tpu as pltpu
from jax.sharding import Mesh
from jax.sharding import PartitionSpec as P

BETA_ONE = 0.9
BETA_TWO = 0.95
EPSILON = 1e-08
STEP_SCALE = 0.5

Z_HI, Z_LO, X_HI, CORE = 8, 2, 2, 2
DP = ("z_hi", "z_lo", "x_hi", "core")
TENSOR = 8
TILE = 256
TOKEN_TILE = 256


def dot(lhs, rhs, lhs_dim, rhs_dim):
    return lax.dot_general(
        lhs,
        rhs,
        (((lhs_dim,), (rhs_dim,)), ((), ())),
        preferred_element_type=jnp.float32,
    )


def scatter_sum(blocks, axes):
    blocks = lax.all_to_all(blocks, axes, 0, 0, tiled=True)
    return jnp.sum(blocks, axis=0)


def spread_rows(value, axes, count):
    copies = jnp.broadcast_to(value[None], (count,) + value.shape)
    return lax.all_to_all(copies, axes, 0, 0, tiled=True)


def swap_cores(value):
    return lax.ppermute(value, "core", [(0, 1), (1, 0)])


def rank_order(rank):
    rows = np.arange(rank).reshape(Z_HI, Z_LO, X_HI, CORE, -1)
    return rows.transpose(3, 2, 1, 0, 4).reshape(-1)


def first_product(turned, acts, where, row_block):
    rank, features = turned.shape
    tokens = acts.shape[0]
    share = rank // (CORE * TENSOR)
    deal = row_block // CORE
    piece = deal // TENSOR

    def kernel(where_ref, turned_ref, acts_ref, out_ref):
        dealt = []
        for c in range(CORE):
            start = pl.multiple_of((where_ref[1] * CORE + c) * row_block, row_block)
            some = turned_ref[:, pl.ds(start, row_block)].astype(jnp.float32).T
            some = jnp.where(where_ref[0] == 0, some[:deal], some[deal:])
            dealt.append(jnp.where(where_ref[2] == 1, some, 0.0))
        for i in range(tokens // TOKEN_TILE):
            part = slice(i * TOKEN_TILE, (i + 1) * TOKEN_TILE)
            value = dot(turned_ref[...], acts_ref[part], 1, 1)
            for c in range(CORE):
                for t in range(TENSOR):
                    top = (c * TENSOR + t) * share
                    low = dealt[c][t * piece : (t + 1) * piece, part]
                    block = jnp.concatenate([value[top : top + share], low], axis=0)
                    out_ref[t, c, :, part] = block

    out = (TENSOR, CORE, share + piece, tokens)
    return pl.pallas_call(
        kernel,
        in_specs=[pl.BlockSpec(memory_space=pltpu.SMEM)]
        + [pl.BlockSpec(memory_space=pltpu.VMEM)] * 2,
        out_specs=pl.BlockSpec(memory_space=pltpu.VMEM),
        out_shape=jax.ShapeDtypeStruct(out, jnp.float32),
        cost_estimate=pl.CostEstimate(
            flops=2 * rank * features * tokens,
            bytes_accessed=2 * (turned.size + acts.size + rank * tokens),
            transcendentals=0,
        ),
        compiler_params=pltpu.CompilerParams(vmem_limit_bytes=14 * 2**20),
    )(where, turned, acts)


def sum_and_copy(blocks):
    senders, cores, rows, columns = blocks.shape

    def kernel(in_ref, out_ref):
        for c in range(cores):
            total = in_ref[0, c]
            for t in range(1, senders):
                total += in_ref[t, c]
            total = total.astype(jnp.bfloat16)
            for t in range(senders):
                out_ref[c * senders + t] = total

    return pl.pallas_call(
        kernel,
        in_specs=[pl.BlockSpec(memory_space=pltpu.VMEM)],
        out_specs=pl.BlockSpec(memory_space=pltpu.VMEM),
        out_shape=jax.ShapeDtypeStruct((cores * senders, rows, columns), jnp.bfloat16),
        cost_estimate=pl.CostEstimate(
            flops=blocks.size, bytes_accessed=4 * blocks.size, transcendentals=0
        ),
        compiler_params=pltpu.CompilerParams(vmem_limit_bytes=12 * 2**20),
    )(blocks)


def rank_product(both, cotangent, partner_cotangent, core, share):
    blocks, rows, tokens = both.shape
    columns = cotangent.shape[1]
    count = blocks // CORE

    def kernel(core_ref, both_ref, own_ref, partner_ref, out_ref):
        me = core_ref[0]
        ours = both_ref[pl.ds(me * count, count), :share, :]
        theirs = both_ref[pl.ds((1 - me) * count, count), :share, :]
        ours = ours.reshape(count * share, tokens)
        theirs = theirs.reshape(count * share, tokens)
        for start in range(0, columns, TILE):
            part = slice(start, start + TILE)
            total = dot(ours, own_ref[:, part], 1, 0)
            total += dot(theirs, partner_ref[:, part], 1, 0)
            out_ref[:, part] = total

    return pl.pallas_call(
        kernel,
        in_specs=[pl.BlockSpec(memory_space=pltpu.SMEM)]
        + [pl.BlockSpec(memory_space=pltpu.VMEM)] * 3,
        out_specs=pl.BlockSpec(memory_space=pltpu.VMEM),
        out_shape=jax.ShapeDtypeStruct((count * share, columns), jnp.float32),
        cost_estimate=pl.CostEstimate(
            flops=4 * count * share * tokens * columns,
            bytes_accessed=2 * (both.size + 2 * cotangent.size + count * share * columns),
            transcendentals=0,
        ),
        compiler_params=pltpu.CompilerParams(vmem_limit_bytes=12 * 2**20),
    )(core.astype(jnp.int32).reshape(1), both, cotangent, partner_cotangent)


def local(acts, cotangent, basis, weight, first_moment, second_moment):
    rank = basis.shape[1]
    half = rank // 2
    core = lax.axis_index("core")
    share = half // TENSOR
    columns = cotangent.shape[1]
    row_block = weight.shape[0]
    place = jnp.asarray(np.eye(rank)[rank_order(rank)], jnp.bfloat16)

    spot = lax.axis_index("z_lo") * X_HI + lax.axis_index("x_hi")
    mine = lax.axis_index("tensor") == lax.axis_index("z_hi")
    where = jnp.stack([core, spot, mine.astype(jnp.int32)]).astype(jnp.int32)
    turned = dot(place, basis, 1, 1).astype(jnp.bfloat16)
    both = first_product(turned, acts, where, row_block)
    both = lax.all_to_all(both, "tensor", 0, 0, tiled=True)
    both, cotangent = lax.optimization_barrier((both, cotangent))

    partner_cotangent = swap_cores(cotangent)
    both = sum_and_copy(both)
    both = lax.all_to_all(both, ("core", "tensor"), 0, 0, tiled=True)
    row_basis = both[:, share:].reshape(row_block, rank)

    low_grad = rank_product(both, cotangent, partner_cotangent, core, share)
    low_grad = low_grad.reshape(Z_LO * X_HI, -1, columns)
    low_grad = scatter_sum(low_grad, ("x_hi", "z_lo"))
    low_grad = low_grad.reshape(Z_HI, -1, columns)
    low_grad = scatter_sum(low_grad, "z_hi")

    first_new = BETA_ONE * first_moment + (1.0 - BETA_ONE) * low_grad
    second_new = BETA_TWO * second_moment + (1.0 - BETA_TWO) * low_grad * low_grad
    normed = (first_new / (jnp.sqrt(second_new) + EPSILON)).astype(jnp.bfloat16)

    normed = spread_rows(normed, "z_hi", Z_HI).reshape(-1, columns)
    normed = spread_rows(normed, ("x_hi", "z_lo"), Z_LO * X_HI).reshape(half, columns)
    other = swap_cores(normed)
    own_basis = lax.dynamic_slice_in_dim(row_basis, core * half, half, 1)
    other_basis = lax.dynamic_slice_in_dim(row_basis, (1 - core) * half, half, 1)
    update = dot(own_basis, normed, 1, 0) + dot(other_basis, other, 1, 0)
    new_weight = (weight.astype(jnp.float32) - STEP_SCALE * update).astype(jnp.bfloat16)
    return (new_weight, first_new, second_new)


def solution(mesh):
    devices = mesh.devices.reshape(Z_HI, Z_LO, X_HI, CORE, TENSOR)
    split = Mesh(devices, DP + ("tensor",))
    placed = (
        P(DP, "tensor"),
        P(DP, "tensor"),
        P("tensor", None),
        P(DP, "tensor"),
        P(DP, "tensor"),
        P(DP, "tensor"),
    )
    return jax.shard_map(
        local,
        mesh=split,
        in_specs=placed,
        out_specs=(P(DP, "tensor"), P(DP, "tensor"), P(DP, "tensor")),
        check_vma=False,
    )
```

```python
import jax
import jax.numpy as jnp
import numpy as np
from jax import lax
from jax.experimental import pallas as pl
from jax.experimental.pallas import tpu as pltpu
from jax.sharding import Mesh
from jax.sharding import PartitionSpec as P

BETA_ONE = 0.9
BETA_TWO = 0.95
EPSILON = 1e-08
STEP_SCALE = 0.5

Z_HI, Z_LO, X_HI, CORE = 8, 2, 2, 2
DP = ("z_hi", "z_lo", "x_hi", "core")
TENSOR = 8
TILE = 256
TOKEN_TILE = 512


def dot(lhs, rhs, lhs_dim, rhs_dim):
    return lax.dot_general(
        lhs,
        rhs,
        (((lhs_dim,), (rhs_dim,)), ((), ())),
        preferred_element_type=jnp.float32,
    )


def scatter_sum(blocks, axes):
    blocks = lax.all_to_all(blocks, axes, 0, 0, tiled=True)
    return jnp.sum(blocks.astype(jnp.float32), axis=0)


def spread_rows(value, axes, count):
    copies = jnp.broadcast_to(value[None], (count,) + value.shape)
    return lax.all_to_all(copies, axes, 0, 0, tiled=True)


def swap_cores(value):
    return lax.ppermute(value, "core", [(0, 1), (1, 0)])


def rank_order(rank):
    rows = np.arange(rank).reshape(Z_HI, Z_LO, X_HI, CORE, -1)
    return rows.transpose(3, 2, 1, 0, 4).reshape(-1)


def first_product(turned, acts, where, row_block):
    rank, features = turned.shape
    tokens = acts.shape[0]
    share = rank // (CORE * TENSOR)
    deal = row_block // CORE
    piece = deal // TENSOR

    def kernel(where_ref, turned_ref, acts_ref, out_ref):
        dealt = []
        for c in range(CORE):
            start = pl.multiple_of((where_ref[1] * CORE + c) * row_block, row_block)
            some = turned_ref[:, pl.ds(start, row_block)].astype(jnp.float32).T
            some = jnp.where(where_ref[0] == 0, some[:deal], some[deal:])
            dealt.append(jnp.where(where_ref[2] == 1, some, 0.0))
        for i in range(tokens // TOKEN_TILE):
            part = slice(i * TOKEN_TILE, (i + 1) * TOKEN_TILE)
            value = dot(turned_ref[...], acts_ref[part], 1, 1)
            for c in range(CORE):
                for t in range(TENSOR):
                    top = (c * TENSOR + t) * share
                    low = dealt[c][t * piece : (t + 1) * piece, part]
                    block = jnp.concatenate([value[top : top + share], low], axis=0)
                    out_ref[t, c, :, part] = block.astype(jnp.bfloat16)

    out = (TENSOR, CORE, share + piece, tokens)
    return pl.pallas_call(
        kernel,
        in_specs=[pl.BlockSpec(memory_space=pltpu.SMEM)]
        + [pl.BlockSpec(memory_space=pltpu.VMEM)] * 2,
        out_specs=pl.BlockSpec(memory_space=pltpu.VMEM),
        out_shape=jax.ShapeDtypeStruct(out, jnp.bfloat16),
        cost_estimate=pl.CostEstimate(
            flops=2 * rank * features * tokens,
            bytes_accessed=2 * (turned.size + acts.size + rank * tokens),
            transcendentals=0,
        ),
        compiler_params=pltpu.CompilerParams(vmem_limit_bytes=14 * 2**20),
    )(where, turned, acts)


def sum_and_copy(blocks):
    senders, cores, rows, columns = blocks.shape

    def kernel(in_ref, out_ref):
        for c in range(cores):
            total = in_ref[0, c].astype(jnp.float32)
            for t in range(1, senders):
                total += in_ref[t, c].astype(jnp.float32)
            total = total.astype(jnp.bfloat16)
            for t in range(senders):
                out_ref[c * senders + t] = total

    return pl.pallas_call(
        kernel,
        in_specs=[pl.BlockSpec(memory_space=pltpu.VMEM)],
        out_specs=pl.BlockSpec(memory_space=pltpu.VMEM),
        out_shape=jax.ShapeDtypeStruct((cores * senders, rows, columns), jnp.bfloat16),
        cost_estimate=pl.CostEstimate(
            flops=blocks.size, bytes_accessed=4 * blocks.size, transcendentals=0
        ),
        compiler_params=pltpu.CompilerParams(vmem_limit_bytes=8 * 2**20),
    )(blocks)


def rank_product(both, cotangent, partner_cotangent, core, share):
    blocks, rows, tokens = both.shape
    columns = cotangent.shape[1]
    count = blocks // CORE

    def kernel(core_ref, both_ref, own_ref, partner_ref, out_ref):
        me = core_ref[0]
        ours = both_ref[pl.ds(me * count, count), :share, :]
        theirs = both_ref[pl.ds((1 - me) * count, count), :share, :]
        ours = ours.reshape(count * share, tokens)
        theirs = theirs.reshape(count * share, tokens)
        for start in range(0, columns, TILE):
            part = slice(start, start + TILE)
            total = dot(ours, own_ref[:, part], 1, 0)
            total += dot(theirs, partner_ref[:, part], 1, 0)
            out_ref[:, part] = total.astype(jnp.bfloat16)

    return pl.pallas_call(
        kernel,
        in_specs=[pl.BlockSpec(memory_space=pltpu.SMEM)]
        + [pl.BlockSpec(memory_space=pltpu.VMEM)] * 3,
        out_specs=pl.BlockSpec(memory_space=pltpu.VMEM),
        out_shape=jax.ShapeDtypeStruct((count * share, columns), jnp.bfloat16),
        cost_estimate=pl.CostEstimate(
            flops=4 * count * share * tokens * columns,
            bytes_accessed=2 * (both.size + 2 * cotangent.size + count * share * columns),
            transcendentals=0,
        ),
        compiler_params=pltpu.CompilerParams(vmem_limit_bytes=12 * 2**20),
    )(core.astype(jnp.int32).reshape(1), both, cotangent, partner_cotangent)


def adam_step(blocks, first_moment, second_moment):
    count, rows, columns = blocks.shape

    def kernel(in_ref, first_ref, second_ref, copies_ref, first_out, second_out):
        low_grad = in_ref[0].astype(jnp.float32)
        for i in range(1, count):
            low_grad += in_ref[i].astype(jnp.float32)
        first_new = BETA_ONE * first_ref[...] + (1.0 - BETA_ONE) * low_grad
        second_new = BETA_TWO * second_ref[...] + (1.0 - BETA_TWO) * low_grad * low_grad
        first_out[...] = first_new
        second_out[...] = second_new
        normed = (first_new / (jnp.sqrt(second_new) + EPSILON)).astype(jnp.bfloat16)
        for i in range(count):
            copies_ref[i] = normed

    vmem = pl.BlockSpec(memory_space=pltpu.VMEM)
    return pl.pallas_call(
        kernel,
        in_specs=[vmem] * 3,
        out_specs=[vmem] * 3,
        out_shape=[
            jax.ShapeDtypeStruct(blocks.shape, jnp.bfloat16),
            jax.ShapeDtypeStruct((rows, columns), jnp.float32),
            jax.ShapeDtypeStruct((rows, columns), jnp.float32),
        ],
        cost_estimate=pl.CostEstimate(
            flops=20 * blocks.size, bytes_accessed=4 * blocks.size, transcendentals=0
        ),
        compiler_params=pltpu.CompilerParams(vmem_limit_bytes=8 * 2**20),
    )(blocks, first_moment, second_moment)


def local(acts, cotangent, basis, weight, first_moment, second_moment):
    rank = basis.shape[1]
    half = rank // 2
    core = lax.axis_index("core")
    share = half // TENSOR
    columns = cotangent.shape[1]
    row_block = weight.shape[0]
    place = jnp.asarray(np.eye(rank)[rank_order(rank)], jnp.bfloat16)

    spot = lax.axis_index("z_lo") * X_HI + lax.axis_index("x_hi")
    mine = lax.axis_index("tensor") == lax.axis_index("z_hi")
    where = jnp.stack([core, spot, mine.astype(jnp.int32)]).astype(jnp.int32)
    turned = dot(place, basis, 1, 1).astype(jnp.bfloat16)
    both = first_product(turned, acts, where, row_block)
    both = lax.all_to_all(both, "tensor", 0, 0, tiled=True)
    both, cotangent = lax.optimization_barrier((both, cotangent))

    partner_cotangent = swap_cores(cotangent)
    both = sum_and_copy(both)
    both = lax.all_to_all(both, ("core", "tensor"), 0, 0, tiled=True)
    row_basis = both[:, share:].reshape(row_block, rank)

    low_grad = rank_product(both, cotangent, partner_cotangent, core, share)
    low_grad = low_grad.reshape(Z_LO * X_HI, -1, columns)
    low_grad = scatter_sum(low_grad, ("x_hi", "z_lo"))
    low_grad = low_grad.astype(jnp.bfloat16).reshape(Z_HI, -1, columns)
    blocks = lax.all_to_all(low_grad, "z_hi", 0, 0, tiled=True)
    copies, first_new, second_new = adam_step(blocks, first_moment, second_moment)
    normed = lax.all_to_all(copies, "z_hi", 0, 0, tiled=True).reshape(-1, columns)
    normed = spread_rows(normed, ("x_hi", "z_lo"), Z_LO * X_HI).reshape(half, columns)
    other = swap_cores(normed)
    own_basis = lax.dynamic_slice_in_dim(row_basis, core * half, half, 1)
    other_basis = lax.dynamic_slice_in_dim(row_basis, (1 - core) * half, half, 1)
    update = dot(own_basis, normed, 1, 0) + dot(other_basis, other, 1, 0)
    new_weight = (weight.astype(jnp.float32) - STEP_SCALE * update).astype(jnp.bfloat16)
    return (new_weight, first_new, second_new)


def solution(mesh):
    devices = mesh.devices.reshape(Z_HI, Z_LO, X_HI, CORE, TENSOR)
    split = Mesh(devices, DP + ("tensor",))
    placed = (
        P(DP, "tensor"),
        P(DP, "tensor"),
        P("tensor", None),
        P(DP, "tensor"),
        P(DP, "tensor"),
        P(DP, "tensor"),
    )
    return jax.shard_map(
        local,
        mesh=split,
        in_specs=placed,
        out_specs=(P(DP, "tensor"), P(DP, "tensor"), P(DP, "tensor")),
        check_vma=False,
    )
```

```python
import jax
import jax.numpy as jnp
import numpy as np
from jax import lax
from jax.experimental import pallas as pl
from jax.experimental.pallas import tpu as pltpu
from jax.sharding import Mesh
from jax.sharding import PartitionSpec as P

BETA_ONE = 0.9
BETA_TWO = 0.95
EPSILON = 1e-08
STEP_SCALE = 0.5

Z_HI, Z_LO, X_HI, CORE = 8, 2, 2, 2
DP = ("z_hi", "z_lo", "x_hi", "core")
TENSOR = 8
TILE = 256
TOKEN_TILE = 512


def dot(lhs, rhs, lhs_dim, rhs_dim):
    return lax.dot_general(
        lhs,
        rhs,
        (((lhs_dim,), (rhs_dim,)), ((), ())),
        preferred_element_type=jnp.float32,
    )


def scatter_sum(blocks, axes):
    blocks = lax.all_to_all(blocks, axes, 0, 0, tiled=True)
    return jnp.sum(blocks.astype(jnp.float32), axis=0)


def spread_rows(value, axes, count):
    copies = jnp.broadcast_to(value[None], (count,) + value.shape)
    return lax.all_to_all(copies, axes, 0, 0, tiled=True)


def swap_cores(value):
    return lax.ppermute(value, "core", [(0, 1), (1, 0)])


def rank_order(rank):
    rows = np.arange(rank).reshape(Z_HI, Z_LO, X_HI, CORE, -1)
    return rows.transpose(3, 2, 1, 0, 4).reshape(-1)


def first_product(turned, acts, where, row_block):
    rank, features = turned.shape
    tokens = acts.shape[0]
    share = rank // (CORE * TENSOR)
    deal = row_block // CORE
    piece = deal // TENSOR

    def kernel(where_ref, turned_ref, acts_ref, out_ref):
        dealt = []
        for c in range(CORE):
            start = pl.multiple_of((where_ref[1] * CORE + c) * row_block, row_block)
            some = turned_ref[:, pl.ds(start, row_block)].astype(jnp.float32).T
            some = jnp.where(where_ref[0] == 0, some[:deal], some[deal:])
            dealt.append(jnp.where(where_ref[2] == 1, some, 0.0))
        for i in range(tokens // TOKEN_TILE):
            part = slice(i * TOKEN_TILE, (i + 1) * TOKEN_TILE)
            value = dot(turned_ref[...], acts_ref[part], 1, 1)
            for c in range(CORE):
                for t in range(TENSOR):
                    top = (c * TENSOR + t) * share
                    low = dealt[c][t * piece : (t + 1) * piece, part]
                    block = jnp.concatenate([value[top : top + share], low], axis=0)
                    out_ref[t, c, :, part] = block.astype(jnp.bfloat16)

    out = (TENSOR, CORE, share + piece, tokens)
    return pl.pallas_call(
        kernel,
        in_specs=[pl.BlockSpec(memory_space=pltpu.SMEM)]
        + [pl.BlockSpec(memory_space=pltpu.VMEM)] * 2,
        out_specs=pl.BlockSpec(memory_space=pltpu.VMEM),
        out_shape=jax.ShapeDtypeStruct(out, jnp.bfloat16),
        cost_estimate=pl.CostEstimate(
            flops=2 * rank * features * tokens,
            bytes_accessed=2 * (turned.size + acts.size + rank * tokens),
            transcendentals=0,
        ),
        compiler_params=pltpu.CompilerParams(vmem_limit_bytes=14 * 2**20),
    )(where, turned, acts)


def sum_and_copy(blocks):
    senders, cores, rows, columns = blocks.shape

    def kernel(in_ref, out_ref):
        for c in range(cores):
            total = in_ref[0, c].astype(jnp.float32)
            for t in range(1, senders):
                total += in_ref[t, c].astype(jnp.float32)
            total = total.astype(jnp.bfloat16)
            for t in range(senders):
                out_ref[c * senders + t] = total

    return pl.pallas_call(
        kernel,
        in_specs=[pl.BlockSpec(memory_space=pltpu.VMEM)],
        out_specs=pl.BlockSpec(memory_space=pltpu.VMEM),
        out_shape=jax.ShapeDtypeStruct((cores * senders, rows, columns), jnp.bfloat16),
        cost_estimate=pl.CostEstimate(
            flops=blocks.size, bytes_accessed=4 * blocks.size, transcendentals=0
        ),
        compiler_params=pltpu.CompilerParams(vmem_limit_bytes=8 * 2**20),
    )(blocks)


def rank_product(both, cotangent, partner_cotangent, core, share):
    blocks, rows, tokens = both.shape
    columns = cotangent.shape[1]
    count = blocks // CORE

    def kernel(core_ref, both_ref, own_ref, partner_ref, out_ref):
        me = core_ref[0]
        ours = both_ref[pl.ds(me * count, count), :share, :]
        theirs = both_ref[pl.ds((1 - me) * count, count), :share, :]
        ours = ours.reshape(count * share, tokens)
        theirs = theirs.reshape(count * share, tokens)
        for start in range(0, columns, TILE):
            part = slice(start, start + TILE)
            total = dot(ours, own_ref[:, part], 1, 0)
            total += dot(theirs, partner_ref[:, part], 1, 0)
            out_ref[:, part] = total.astype(jnp.bfloat16)

    return pl.pallas_call(
        kernel,
        in_specs=[pl.BlockSpec(memory_space=pltpu.SMEM)]
        + [pl.BlockSpec(memory_space=pltpu.VMEM)] * 3,
        out_specs=pl.BlockSpec(memory_space=pltpu.VMEM),
        out_shape=jax.ShapeDtypeStruct((count * share, columns), jnp.bfloat16),
        cost_estimate=pl.CostEstimate(
            flops=4 * count * share * tokens * columns,
            bytes_accessed=2 * (both.size + 2 * cotangent.size + count * share * columns),
            transcendentals=0,
        ),
        compiler_params=pltpu.CompilerParams(vmem_limit_bytes=12 * 2**20),
    )(core.astype(jnp.int32).reshape(1), both, cotangent, partner_cotangent)


def adam_step(blocks, first_moment, second_moment):
    count, rows, columns = blocks.shape

    def kernel(in_ref, first_ref, second_ref, copies_ref, first_out, second_out):
        low_grad = in_ref[0].astype(jnp.float32)
        for i in range(1, count):
            low_grad += in_ref[i].astype(jnp.float32)
        first_new = BETA_ONE * first_ref[...] + (1.0 - BETA_ONE) * low_grad
        second_new = BETA_TWO * second_ref[...] + (1.0 - BETA_TWO) * low_grad * low_grad
        first_out[...] = first_new
        second_out[...] = second_new
        normed = (first_new / (jnp.sqrt(second_new) + EPSILON)).astype(jnp.bfloat16)
        for i in range(count):
            copies_ref[i] = normed

    vmem = pl.BlockSpec(memory_space=pltpu.VMEM)
    return pl.pallas_call(
        kernel,
        in_specs=[vmem] * 3,
        out_specs=[vmem] * 3,
        out_shape=[
            jax.ShapeDtypeStruct(blocks.shape, jnp.bfloat16),
            jax.ShapeDtypeStruct((rows, columns), jnp.float32),
            jax.ShapeDtypeStruct((rows, columns), jnp.float32),
        ],
        cost_estimate=pl.CostEstimate(
            flops=20 * blocks.size, bytes_accessed=4 * blocks.size, transcendentals=0
        ),
        compiler_params=pltpu.CompilerParams(vmem_limit_bytes=8 * 2**20),
    )(blocks, first_moment, second_moment)


def local(acts, cotangent, basis, weight, first_moment, second_moment):
    rank = basis.shape[1]
    half = rank // 2
    core = lax.axis_index("core")
    share = half // TENSOR
    columns = cotangent.shape[1]
    row_block = weight.shape[0]
    place = jnp.asarray(np.eye(rank)[rank_order(rank)], jnp.bfloat16)

    spot = lax.axis_index("z_lo") * X_HI + lax.axis_index("x_hi")
    mine = lax.axis_index("tensor") == lax.axis_index("z_hi")
    where = jnp.stack([core, spot, mine.astype(jnp.int32)]).astype(jnp.int32)
    turned = dot(place, basis, 1, 1).astype(jnp.bfloat16)
    both = first_product(turned, acts, where, row_block)
    both = lax.all_to_all(both, "tensor", 0, 0, tiled=True)
    both = sum_and_copy(both)
    both, cotangent = lax.optimization_barrier((both, cotangent))

    partner_cotangent = swap_cores(cotangent)
    both = lax.all_to_all(both, ("core", "tensor"), 0, 0, tiled=True)
    row_basis = both[:, share:].reshape(row_block, rank)

    low_grad = rank_product(both, cotangent, partner_cotangent, core, share)
    low_grad = low_grad.reshape(Z_LO * X_HI, -1, columns)
    low_grad = scatter_sum(low_grad, ("x_hi", "z_lo"))
    low_grad = low_grad.astype(jnp.bfloat16).reshape(Z_HI, -1, columns)
    blocks = lax.all_to_all(low_grad, "z_hi", 0, 0, tiled=True)
    copies, first_new, second_new = adam_step(blocks, first_moment, second_moment)
    normed = lax.all_to_all(copies, "z_hi", 0, 0, tiled=True).reshape(-1, columns)
    normed = spread_rows(normed, ("x_hi", "z_lo"), Z_LO * X_HI).reshape(half, columns)
    other = swap_cores(normed)
    own_basis = lax.dynamic_slice_in_dim(row_basis, core * half, half, 1)
    other_basis = lax.dynamic_slice_in_dim(row_basis, (1 - core) * half, half, 1)
    update = dot(own_basis, normed, 1, 0) + dot(other_basis, other, 1, 0)
    new_weight = (weight.astype(jnp.float32) - STEP_SCALE * update).astype(jnp.bfloat16)
    return (new_weight, first_new, second_new)


def solution(mesh):
    devices = mesh.devices.reshape(Z_HI, Z_LO, X_HI, CORE, TENSOR)
    split = Mesh(devices, DP + ("tensor",))
    placed = (
        P(DP, "tensor"),
        P(DP, "tensor"),
        P("tensor", None),
        P(DP, "tensor"),
        P(DP, "tensor"),
        P(DP, "tensor"),
    )
    return jax.shard_map(
        local,
        mesh=split,
        in_specs=placed,
        out_specs=(P(DP, "tensor"), P(DP, "tensor"), P(DP, "tensor")),
        check_vma=False,
    )
```
